256 devices in a mesh: tile: 64 (over x, z, core), pair: 4 (over y).
Axes of the slice: x: 4, y: 4, z: 8, core: 2. Of those that a mesh axis runs over, the one named last changes fastest.
Arguments:
- amplitudes: bfloat16 [64, 3072, 1024], P('tile', 'pair'), may hold values from -6 to 6
- integrals: bfloat16 [64, 4, 1024, 1024], P('tile', None, 'pair'), may hold values from -0.09375 to 0.09375
- residual_in: float32 [64, 3072, 1024], P('tile', 'pair'), may hold values from -6 to 6
- shape_cols: int32 [64, 4], P('tile'), may hold values from -1 to 63, as said below
Outputs:
- residual_out: float32 [64, 3072, 1024], P('tile', 'pair')
The draws below stay inside these ranges and needn't reach their ends.
Inputs may be any that keep to these rules, and one draw needn't show every extreme that they name: `shape_cols`: row p lists p itself first, then 4 - 1 distinct tile pairs p + o with 0 < |o| <= 2, where a tile pair outside 0 to 63 is written -1.
All inputs are finite; a program needn't handle non-finite values.
Results may differ from the reference program's by a relative error of at most 0.0003.
Values may be sent and summed in bfloat16 or wider, within the bound.
No kernel may reach another device: no remote copies, remote signals or barrier semaphores. Data moves between devices by JAX's collectives and lax.ppermute only.
A program may use at most 128 MiB of HBM per device.

```python
import jax
import jax.numpy as jnp
import numpy as np
from jax import lax

INDEX_PAIRS = 1024
OCC = 3072
TILE_PAIR_COUNT = 64
BLOCKS_PER_PAIR = 4
REACH = 2


def draw_shape_cols(key, part):
    key = jax.random.fold_in(key, 11)
    remaining_tiles = jnp.array(np.array([o for o in range(-REACH, REACH + 1) if o != 0], dtype=np.int32))
    block_ordering = jax.vmap(lambda k: jax.random.permutation(k, 2 * REACH))(jax.random.split(key, TILE_PAIR_COUNT))
    chosen_blocks = remaining_tiles[block_ordering[:, :BLOCKS_PER_PAIR - 1]]
    rowids = jnp.arange(TILE_PAIR_COUNT, dtype=jnp.int32)
    coupled = rowids[:, None] + chosen_blocks
    coupled = jnp.where((coupled >= 0) & (coupled < TILE_PAIR_COUNT), coupled, -1)
    return jnp.concatenate([rowids[:, None], coupled], axis=1).astype(jnp.int32)


def block_levels(stream_key, extent, shards, least, largest):
    gain = 1.0
    for dim, parts in shards:
        heights = jax.random.uniform(jax.random.fold_in(jax.random.fold_in(stream_key, 6), dim), (parts,), jnp.float32, least / len(shards), largest / len(shards))
        gain = gain * jnp.repeat(jnp.exp(heights), extent[dim] // parts).reshape((-1,) + (1,) * (len(extent) - 1 - dim))
    return gain


def gaussian(rng, shape, deviation, most, cuts=(), kind=jnp.bfloat16):
    gain = block_levels(rng, shape, cuts, -0.22, 0.18) if cuts else 1.0
    values = jax.random.normal(rng, shape, jnp.float32) * deviation * gain
    return jnp.minimum(jnp.maximum(values, -most), most).astype(kind)


def setup_inputs(seed: int = 0) -> dict:
    seeds = jax.random.split(jax.random.key(seed), 5)
    return {
        "amplitudes": gaussian(seeds[0], (TILE_PAIR_COUNT, OCC, INDEX_PAIRS), 1.0, 6.0, ((0, 64), (1, 4))),
        "integrals": gaussian(seeds[1], (TILE_PAIR_COUNT, BLOCKS_PER_PAIR, INDEX_PAIRS, INDEX_PAIRS), (INDEX_PAIRS * BLOCKS_PER_PAIR) ** -0.5, 0.09375, ((0, 64), (2, 4))),
        "residual_in": gaussian(seeds[2], (TILE_PAIR_COUNT, OCC, INDEX_PAIRS), 1.0, 6.0, ((0, 64), (1, 4)), jnp.float32),
        "shape_cols": draw_shape_cols(jax.random.fold_in(seeds[4], 71), 0),
    }


def reference(amplitudes, integrals, residual_in, shape_cols):
    def one_row(packed):
        blocks, columns, previous = packed
        present = (columns >= 0).astype(jnp.float32)
        clipped = jnp.clip(columns, 0, TILE_PAIR_COUNT - 1).astype(jnp.int32)
        coupled = amplitudes[clipped].astype(jnp.float32) * present[:, None, None]
        ladder = jnp.einsum("sic,scd->id", coupled, blocks.astype(jnp.float32))
        return previous + ladder

    return lax.map(one_row, (integrals, shape_cols, residual_in))
```

```python
import jax
import jax.numpy as jnp
from jax import lax
from jax.experimental import pallas as pl
from jax.experimental.pallas import tpu as pltpu
from jax.sharding import PartitionSpec as P

REACH = 2
SLOTS = 4
MIB = 1024 * 1024
VMEM = pl.BlockSpec(memory_space=pltpu.VMEM)
SMEM = pl.BlockSpec(memory_space=pltpu.SMEM)
ANY = pl.BlockSpec(memory_space=pl.ANY)


def shifted(block, axis, distance):
    devices = range(lax.axis_size(axis))
    route = [(i - distance, i) for i in devices if i - distance in devices]
    return lax.ppermute(block, axis, route)


def turned(block, axis, distance):
    size = lax.axis_size(axis)
    return lax.ppermute(block, axis, [(i, (i + distance) % size) for i in range(size)])


def near_kernel(below, above, mine, low2, low1, own, high1, high2, residual, listed, total, kept, chosen):
    rows = residual.shape[0]
    width = mine.shape[1]
    myself = lax.axis_index("tile")
    pair = lax.axis_index("pair")
    nothing = jnp.where(myself < REACH, 0, 2 * REACH)

    for slot in range(SLOTS):
        column = listed[0, slot]
        place = jnp.where(column >= 0, jnp.clip(column - myself + REACH, 0, 2 * REACH), nothing)
        for index, source in enumerate((low2, low1, own, high1, high2)):

            @pl.when(place == index)
            def _():
                for turn, step in enumerate((0, -1, 1, 2)):
                    begin = pl.multiple_of(lax.rem(pair + 4 + step, 4) * width, width)
                    part = source[:, pl.ds(begin, width)]
                    if turn < 3:
                        chosen[turn, :, slot * width : (slot + 1) * width] = part
                    else:
                        kept[:, slot * width : (slot + 1) * width] = part

    lanes = 256
    for begin in range(0, residual.shape[1], lanes):
        value = residual[:, begin : begin + lanes]
        for turn, shard in enumerate((mine, below, above)):
            right = shard[:, :, begin : begin + lanes].reshape(SLOTS * width, lanes)
            value += jnp.dot(chosen[turn], right, preferred_element_type=jnp.float32)
        total[:, begin : begin + lanes] = value


def far_kernel(first, second, total, kept, out, staged, sems):
    width = first.shape[1]
    half = first.shape[0] * width
    lanes = 256
    copies = []
    for tile in range(total.shape[1] // lanes):
        here = slice(tile * lanes, (tile + 1) * lanes)
        value = jnp.dot(kept[:, :half], first[:, :, here].reshape(half, lanes), preferred_element_type=jnp.float32)
        value += jnp.dot(kept[:, half:], second[:, :, here].reshape(half, lanes), preferred_element_type=jnp.float32)
        staged[:, here] = total[:, here] + value
        copies.append(pltpu.make_async_copy(staged.at[:, here], out.at[:, here], sems.at[tile]))
        copies[-1].start()
    for copy in copies:
        copy.wait()


def pass_kernel(*refs):
    del refs


def passed(blocks, flops):
    count = len(blocks)
    return pl.pallas_call(
        pass_kernel,
        out_shape=[jax.ShapeDtypeStruct(block.shape, block.dtype) for block in blocks],
        in_specs=[ANY] * count,
        out_specs=[ANY] * count,
        input_output_aliases={index: index for index in range(count)},
        compiler_params=pltpu.CompilerParams(vmem_limit_bytes=MIB),
        cost_estimate=pl.CostEstimate(flops=flops, bytes_accessed=0, transcendentals=0),
    )(*blocks)


def shards(amplitudes, integrals, residual_in, shape_cols):
    own = amplitudes[0]
    mine = integrals[0]
    width, columns = mine.shape[1], mine.shape[2]
    rows = own.shape[0]

    below = turned(mine, "pair", 1)
    above = turned(mine, "pair", -1)
    low1 = shifted(own, "tile", 1)
    high1 = shifted(own, "tile", -1)
    low2 = shifted(low1, "tile", 1)
    high2 = shifted(high1, "tile", -1)
    below, above = passed((below, above), 20000000000)
    far_first = turned(below[:2], "pair", 1)
    far_second = turned(above[2:], "pair", -1)

    total, kept = pl.pallas_call(
        near_kernel,
        out_shape=[
            jax.ShapeDtypeStruct((rows, columns), jnp.float32),
            jax.ShapeDtypeStruct((rows, SLOTS * width), own.dtype),
        ],
        in_specs=[VMEM] * 9 + [SMEM],
        out_specs=[VMEM] * 2,
        scratch_shapes=[pltpu.VMEM((3, rows, SLOTS * width), own.dtype)],
        compiler_params=pltpu.CompilerParams(vmem_limit_bytes=16 * MIB),
        cost_estimate=pl.CostEstimate(flops=1 << 32, bytes_accessed=1 << 20, transcendentals=0),
    )(below, above, mine, low2, low1, own, high1, high2, residual_in[0], shape_cols)
    out = pl.pallas_call(
        far_kernel,
        out_shape=jax.ShapeDtypeStruct((rows, columns), jnp.float32),
        in_specs=[VMEM] * 4,
        out_specs=ANY,
        scratch_shapes=[pltpu.VMEM((rows, columns), jnp.float32), pltpu.SemaphoreType.DMA((4,))],
        compiler_params=pltpu.CompilerParams(vmem_limit_bytes=12 * MIB),
        cost_estimate=pl.CostEstimate(flops=1 << 30, bytes_accessed=1 << 20, transcendentals=0),
    )(far_first, far_second, total, kept)
    return out[None]


def solution(mesh):
    in_specs = (
        P("tile", "pair", None),
        P("tile", None, "pair", None),
        P("tile", "pair", None),
        P("tile", None),
    )
    out_specs = P("tile", "pair", None)
    return jax.shard_map(shards, mesh=mesh, in_specs=in_specs, out_specs=out_specs, check_vma=False)
```

```python
import functools

import jax
import jax.numpy as jnp
from jax import lax
from jax.experimental import pallas as pl
from jax.experimental.pallas import tpu as pltpu
from jax.sharding import PartitionSpec as P

REACH = 2
SLOTS = 4
FRONT = 768
MIB = 1024 * 1024
VMEM = pl.BlockSpec(memory_space=pltpu.VMEM)
SMEM = pl.BlockSpec(memory_space=pltpu.SMEM)
ANY = pl.BlockSpec(memory_space=pl.ANY)


def shifted(block, axis, distance):
    devices = range(lax.axis_size(axis))
    route = [(i - distance, i) for i in devices if i - distance in devices]
    return lax.ppermute(block, axis, route)


def turned(block, axis, distance):
    size = lax.axis_size(axis)
    return lax.ppermute(block, axis, [(i, (i + distance) % size) for i in range(size)])


def near_kernel(below, above, mine, low2, low1, own, high1, high2, residual, listed, total, kept, chosen):
    rows = residual.shape[0]
    width = mine.shape[1]
    myself = lax.axis_index("tile")
    pair = lax.axis_index("pair")
    nothing = jnp.where(myself < REACH, 0, 2 * REACH)

    for slot in range(SLOTS):
        column = listed[0, slot]
        place = jnp.where(column >= 0, jnp.clip(column - myself + REACH, 0, 2 * REACH), nothing)
        for index, source in enumerate((low2, low1, own, high1, high2)):

            @pl.when(place == index)
            def _():
                for turn, step in enumerate((0, -1, 1, 2)):
                    begin = pl.multiple_of(lax.rem(pair + 4 + step, 4) * width, width)
                    part = source[:, pl.ds(begin, width)]
                    if turn < 3:
                        chosen[turn, :, slot * width : (slot + 1) * width] = part
                    else:
                        kept[:, slot * width : (slot + 1) * width] = part

    lanes = 256
    for begin in range(0, residual.shape[1], lanes):
        value = residual[:, begin : begin + lanes]
        for turn, shard in enumerate((mine, below, above)):
            right = shard[:, :, begin : begin + lanes].reshape(SLOTS * width, lanes)
            value += jnp.dot(chosen[turn], right, preferred_element_type=jnp.float32)
        total[:, begin : begin + lanes] = value


def split_kernel(below, above, *pieces):
    half = SLOTS // 2
    for source, begin, (front, back) in ((below, 0, pieces[:2]), (above, half, pieces[2:])):
        front[...] = source[begin : begin + half, :, :FRONT]
        back[...] = source[begin : begin + half, :, FRONT:]


def far_kernel(begin, first, second, total, kept, *rest):
    out, staged, sems = rest[-3:]
    half = first.shape[0] * first.shape[1]
    lanes = 256
    copies = []
    for tile in range(first.shape[2] // lanes):
        piece = slice(tile * lanes, (tile + 1) * lanes)
        here = slice(begin + tile * lanes, begin + (tile + 1) * lanes)
        value = jnp.dot(kept[:, :half], first[:, :, piece].reshape(half, lanes), preferred_element_type=jnp.float32)
        value += jnp.dot(kept[:, half:], second[:, :, piece].reshape(half, lanes), preferred_element_type=jnp.float32)
        staged[:, piece] = total[:, here] + value
        copies.append(pltpu.make_async_copy(staged.at[:, piece], out.at[:, here], sems.at[tile]))
        copies[-1].start()
    for copy in copies:
        copy.wait()


def far_columns(begin, first, second, total, kept, *out):
    rows = total.shape[0]
    width = first.shape[2]
    return pl.pallas_call(
        functools.partial(far_kernel, begin),
        out_shape=jax.ShapeDtypeStruct(total.shape, total.dtype),
        in_specs=[VMEM] * 4 + [ANY] * len(out),
        out_specs=ANY,
        input_output_aliases={4: 0} if out else {},
        scratch_shapes=[pltpu.VMEM((rows, width), jnp.float32), pltpu.SemaphoreType.DMA((4,))],
        compiler_params=pltpu.CompilerParams(vmem_limit_bytes=12 * MIB),
        cost_estimate=pl.CostEstimate(flops=1 << 29, bytes_accessed=1 << 20, transcendentals=0),
    )(first, second, total, kept, *out)


def shards(amplitudes, integrals, residual_in, shape_cols):
    own = amplitudes[0]
    mine = integrals[0]
    width, columns = mine.shape[1], mine.shape[2]
    rows = own.shape[0]

    below = turned(mine, "pair", 1)
    above = turned(mine, "pair", -1)
    low1 = shifted(own, "tile", 1)
    high1 = shifted(own, "tile", -1)
    low2 = shifted(low1, "tile", 1)
    high2 = shifted(high1, "tile", -1)
    half = SLOTS // 2
    front = jax.ShapeDtypeStruct((half, width, FRONT), mine.dtype)
    back = jax.ShapeDtypeStruct((half, width, columns - FRONT), mine.dtype)
    pieces = pl.pallas_call(
        split_kernel,
        out_shape=[front, back, front, back],
        in_specs=[VMEM] * 2,
        out_specs=[VMEM] * 4,
        compiler_params=pltpu.CompilerParams(vmem_limit_bytes=4 * MIB),
        cost_estimate=pl.CostEstimate(flops=20_000_000_000, bytes_accessed=0, transcendentals=0),
    )(below, above)
    first_front, second_front = turned(pieces[0], "pair", 1), turned(pieces[2], "pair", -1)
    first_back, second_back = turned(pieces[1], "pair", 1), turned(pieces[3], "pair", -1)

    total, kept = pl.pallas_call(
        near_kernel,
        out_shape=[
            jax.ShapeDtypeStruct((rows, columns), jnp.float32),
            jax.ShapeDtypeStruct((rows, SLOTS * width), own.dtype),
        ],
        in_specs=[VMEM] * 9 + [SMEM],
        out_specs=[VMEM] * 2,
        scratch_shapes=[pltpu.VMEM((3, rows, SLOTS * width), own.dtype)],
        compiler_params=pltpu.CompilerParams(vmem_limit_bytes=16 * MIB),
        cost_estimate=pl.CostEstimate(flops=1 << 32, bytes_accessed=1 << 20, transcendentals=0),
    )(below, above, mine, low2, low1, own, high1, high2, residual_in[0], shape_cols)
    out = far_columns(0, first_front, second_front, total, kept)
    out = far_columns(FRONT, first_back, second_back, total, kept, out)
    return out[None]


def solution(mesh):
    in_specs = (
        P("tile", "pair", None),
        P("tile", None, "pair", None),
        P("tile", "pair", None),
        P("tile", None),
    )
    out_specs = P("tile", "pair", None)
    return jax.shard_map(shards, mesh=mesh, in_specs=in_specs, out_specs=out_specs, check_vma=False)
```

```python
import functools

import jax
import jax.numpy as jnp
from jax import lax
from jax.experimental import pallas as pl
from jax.experimental.pallas import tpu as pltpu
from jax.sharding import PartitionSpec as P

REACH = 2
SLOTS = 4
FRONT = 768
PARTS = 3
MIB = 1024 * 1024
VMEM = pl.BlockSpec(memory_space=pltpu.VMEM)
SMEM = pl.BlockSpec(memory_space=pltpu.SMEM)
ANY = pl.BlockSpec(memory_space=pl.ANY)


def shifted(block, axis, distance):
    devices = range(lax.axis_size(axis))
    route = [(i - distance, i) for i in devices if i - distance in devices]
    return lax.ppermute(block, axis, route)


def turned(block, axis, distance):
    size = lax.axis_size(axis)
    return lax.ppermute(block, axis, [(i, (i + distance) % size) for i in range(size)])


def near_kernel(below, above, mine, low2, low1, own, high1, high2, residual, listed, total, kept, chosen):
    rows = residual.shape[0]
    width = mine.shape[1]
    myself = lax.axis_index("tile")
    pair = lax.axis_index("pair")
    nothing = jnp.where(myself < REACH, 0, 2 * REACH)

    for slot in range(SLOTS):
        column = listed[0, slot]
        place = jnp.where(column >= 0, jnp.clip(column - myself + REACH, 0, 2 * REACH), nothing)
        for index, source in enumerate((low2, low1, own, high1, high2)):

            @pl.when(place == index)
            def _():
                for turn, step in enumerate((0, -1, 1, 2)):
                    begin = pl.multiple_of(lax.rem(pair + 4 + step, 4) * width, width)
                    part = source[:, pl.ds(begin, width)]
                    if turn < 3:
                        chosen[turn, :, slot * width : (slot + 1) * width] = part
                    else:
                        kept[:, slot * width : (slot + 1) * width] = part

    lanes = 256
    for begin in range(0, residual.shape[1], lanes):
        value = residual[:, begin : begin + lanes]
        for turn, shard in enumerate((mine, below, above)):
            right = shard[:, :, begin : begin + lanes].reshape(SLOTS * width, lanes)
            value += jnp.dot(chosen[turn], right, preferred_element_type=jnp.float32)
        total[:, begin : begin + lanes] = value


def split_kernel(begin, source, front, back):
    half = SLOTS // 2
    front[...] = source[begin : begin + half, :, :FRONT]
    back[...] = source[begin : begin + half, :, FRONT:]


def split(begin, source, flops):
    half, width, columns = SLOTS // 2, source.shape[1], source.shape[2]
    return pl.pallas_call(
        functools.partial(split_kernel, begin),
        out_shape=[
            jax.ShapeDtypeStruct((half, width, FRONT), source.dtype),
            jax.ShapeDtypeStruct((half, width, columns - FRONT), source.dtype),
        ],
        in_specs=[VMEM],
        out_specs=[VMEM] * 2,
        compiler_params=pltpu.CompilerParams(vmem_limit_bytes=4 * MIB),
        cost_estimate=pl.CostEstimate(flops=flops, bytes_accessed=0, transcendentals=0),
    )(source)


def far_kernel(begin, first, second, total, kept, *rest):
    out, staged, sems = rest[-3:]
    rows, width = staged.shape
    half = first.shape[0] * first.shape[1]
    copies = []
    for tile in range(PARTS):
        here = slice(tile * rows // PARTS, (tile + 1) * rows // PARTS)
        value = jnp.dot(kept[here, :half], first[...].reshape(half, width), preferred_element_type=jnp.float32)
        value += jnp.dot(kept[here, half:], second[...].reshape(half, width), preferred_element_type=jnp.float32)
        staged[here, :] = total[here, begin : begin + width] + value
        copies.append(pltpu.make_async_copy(staged.at[here], out.at[here, begin : begin + width], sems.at[tile]))
        copies[-1].start()
    for copy in copies:
        copy.wait()


def far_columns(begin, first, second, total, kept, *out):
    rows = total.shape[0]
    width = first.shape[2]
    return pl.pallas_call(
        functools.partial(far_kernel, begin),
        out_shape=jax.ShapeDtypeStruct(total.shape, total.dtype),
        in_specs=[VMEM] * 4 + [ANY] * len(out),
        out_specs=ANY,
        input_output_aliases={4: 0} if out else {},
        scratch_shapes=[pltpu.VMEM((rows, width), jnp.float32), pltpu.SemaphoreType.DMA((4,))],
        compiler_params=pltpu.CompilerParams(vmem_limit_bytes=12 * MIB),
        cost_estimate=pl.CostEstimate(flops=1 << 29, bytes_accessed=1 << 20, transcendentals=0),
    )(first, second, total, kept, *out)


def shards(amplitudes, integrals, residual_in, shape_cols):
    own = amplitudes[0]
    mine = integrals[0]
    width, columns = mine.shape[1], mine.shape[2]
    rows = own.shape[0]

    below = turned(mine, "pair", 1)
    above = turned(mine, "pair", -1)
    low1 = shifted(own, "tile", 1)
    high1 = shifted(own, "tile", -1)
    low2 = shifted(low1, "tile", 1)
    high2 = shifted(high1, "tile", -1)
    second_pieces = split(SLOTS // 2, above, 20000000000)
    first_pieces = split(0, below, 0)
    second_front, second_back = (turned(piece, "pair", -1) for piece in second_pieces)
    first_front, first_back = (turned(piece, "pair", 1) for piece in first_pieces)

    total, kept = pl.pallas_call(
        near_kernel,
        out_shape=[
            jax.ShapeDtypeStruct((rows, columns), jnp.float32),
            jax.ShapeDtypeStruct((rows, SLOTS * width), own.dtype),
        ],
        in_specs=[VMEM] * 9 + [SMEM],
        out_specs=[VMEM] * 2,
        scratch_shapes=[pltpu.VMEM((3, rows, SLOTS * width), own.dtype)],
        compiler_params=pltpu.CompilerParams(vmem_limit_bytes=16 * MIB),
        cost_estimate=pl.CostEstimate(flops=1 << 32, bytes_accessed=1 << 20, transcendentals=0),
    )(below, above, mine, low2, low1, own, high1, high2, residual_in[0], shape_cols)
    out = far_columns(0, first_front, second_front, total, kept)
    out = far_columns(FRONT, first_back, second_back, total, kept, out)
    return out[None]


def solution(mesh):
    in_specs = (
        P("tile", "pair", None),
        P("tile", None, "pair", None),
        P("tile", "pair", None),
        P("tile", None),
    )
    out_specs = P("tile", "pair", None)
    return jax.shard_map(shards, mesh=mesh, in_specs=in_specs, out_specs=out_specs, check_vma=False)
```

```python
import functools

import jax
import jax.numpy as jnp
from jax import lax
from jax.experimental import pallas as pl
from jax.experimental.pallas import tpu as pltpu
from jax.sharding import PartitionSpec as P

REACH = 2
SLOTS = 4
FRONT = 768
PARTS = 3
DIRECT = 16
MIB = 1024 * 1024
VMEM = pl.BlockSpec(memory_space=pltpu.VMEM)
SMEM = pl.BlockSpec(memory_space=pltpu.SMEM)
ANY = pl.BlockSpec(memory_space=pl.ANY)


def shifted(block, axis, distance):
    devices = range(lax.axis_size(axis))
    route = [(i - distance, i) for i in devices if i - distance in devices]
    return lax.ppermute(block, axis, route)


def turned(block, axis, distance):
    size = lax.axis_size(axis)
    return lax.ppermute(block, axis, [(i, (i + distance) % size) for i in range(size)])


def near_kernel(straight, below, above, mine, low2, low1, own, high1, high2, residual, listed, total, kept, chosen):
    rows = residual.shape[0]
    width = mine.shape[1]
    myself = lax.axis_index("tile")
    pair = lax.axis_index("pair")
    nothing = jnp.where(myself < REACH, 0, 2 * REACH)

    for slot in range(SLOTS):
        column = listed[0, slot]
        place = jnp.where(column >= 0, jnp.clip(column - myself + REACH, 0, 2 * REACH), nothing)
        for index, source in enumerate((low2, low1, own, high1, high2)):

            @pl.when(place == index)
            def _():
                for turn, step in enumerate((0, -1, 1, 2)):
                    begin = pl.multiple_of(lax.rem(pair + 4 + step, 4) * width, width)
                    part = source[:, pl.ds(begin, width)]
                    if turn < 3:
                        chosen[turn, :, slot * width : (slot + 1) * width] = part
                    else:
                        kept[:, slot * width : (slot + 1) * width] = part

    ends = [kept[:, (slot + 1) * width - DIRECT : (slot + 1) * width] for slot in range(SLOTS)]
    tail = jnp.concatenate(ends, axis=1)
    lanes = 256
    for begin in range(0, residual.shape[1], lanes):
        value = residual[:, begin : begin + lanes]
        for turn, shard in enumerate((mine, below, above)):
            right = shard[:, :, begin : begin + lanes].reshape(SLOTS * width, lanes)
            value += jnp.dot(chosen[turn], right, preferred_element_type=jnp.float32)
        value += jnp.dot(tail, straight[:, :, begin : begin + lanes].reshape(SLOTS * DIRECT, lanes), preferred_element_type=jnp.float32)
        total[:, begin : begin + lanes] = value


def ends_kernel(blocks, out, sems):
    rows = blocks.shape[1]
    copies = []
    for slot in range(SLOTS):
        source = blocks.at[slot, pl.ds(rows - DIRECT, DIRECT)]
        copies.append(pltpu.make_async_copy(source, out.at[slot], sems.at[slot]))
        copies[-1].start()
    for copy in copies:
        copy.wait()


def pass_kernel(given, out):
    del given, out


def passed(block, flops):
    return pl.pallas_call(
        pass_kernel,
        out_shape=jax.ShapeDtypeStruct(block.shape, block.dtype),
        in_specs=[VMEM],
        out_specs=VMEM,
        input_output_aliases={0: 0},
        compiler_params=pltpu.CompilerParams(vmem_limit_bytes=MIB),
        cost_estimate=pl.CostEstimate(flops=flops, bytes_accessed=0, transcendentals=0),
    )(block)


def split_kernel(begin, source, *rest):
    front, back = rest[-2:]
    half = SLOTS // 2
    depth = front.shape[1]
    front[...] = source[begin : begin + half, :depth, :FRONT]
    back[...] = source[begin : begin + half, :depth, FRONT:]


def split(begin, source, flops, *after):
    half, width, columns = SLOTS // 2, source.shape[1], source.shape[2]
    return pl.pallas_call(
        functools.partial(split_kernel, begin),
        out_shape=[
            jax.ShapeDtypeStruct((half, width - DIRECT, FRONT), source.dtype),
            jax.ShapeDtypeStruct((half, width - DIRECT, columns - FRONT), source.dtype),
        ],
        in_specs=[VMEM] + [ANY] * len(after),
        out_specs=[VMEM] * 2,
        compiler_params=pltpu.CompilerParams(vmem_limit_bytes=4 * MIB),
        cost_estimate=pl.CostEstimate(flops=flops, bytes_accessed=0, transcendentals=0),
    )(source, *after)


def far_kernel(begin, first, second, total, kept, *rest):
    out, staged, sems = rest[-3:]
    rows, width = staged.shape
    half, depth = first.shape[:2]
    block = kept.shape[1] // SLOTS
    copies = []
    for tile in range(PARTS):
        here = slice(tile * rows // PARTS, (tile + 1) * rows // PARTS)
        value = 0.0
        for slot in range(SLOTS):
            piece = (first if slot < half else second)[slot % half]
            left = kept[here, slot * block : slot * block + depth]
            value += jnp.dot(left, piece, preferred_element_type=jnp.float32)
        staged[here, :] = total[here, begin : begin + width] + value
        copies.append(pltpu.make_async_copy(staged.at[here], out.at[here, begin : begin + width], sems.at[tile]))
        copies[-1].start()
    for copy in copies:
        copy.wait()


def far_columns(begin, first, second, total, kept, *out):
    rows = total.shape[0]
    width = first.shape[2]
    return pl.pallas_call(
        functools.partial(far_kernel, begin),
        out_shape=jax.ShapeDtypeStruct(total.shape, total.dtype),
        in_specs=[VMEM] * 4 + [ANY] * len(out),
        out_specs=ANY,
        input_output_aliases={4: 0} if out else {},
        scratch_shapes=[pltpu.VMEM((rows, width), jnp.float32), pltpu.SemaphoreType.DMA((4,))],
        compiler_params=pltpu.CompilerParams(vmem_limit_bytes=12 * MIB),
        cost_estimate=pl.CostEstimate(flops=1 << 29, bytes_accessed=1 << 20, transcendentals=0),
    )(first, second, total, kept, *out)


def shards(amplitudes, integrals, residual_in, shape_cols):
    own = amplitudes[0]
    mine = integrals[0]
    width, columns = mine.shape[1], mine.shape[2]
    rows = own.shape[0]

    below = turned(mine, "pair", 1)
    above = turned(mine, "pair", -1)
    ends = pl.pallas_call(
        ends_kernel,
        out_shape=jax.ShapeDtypeStruct((SLOTS, DIRECT, columns), mine.dtype),
        in_specs=[pl.BlockSpec(memory_space=pltpu.HBM)],
        out_specs=VMEM,
        scratch_shapes=[pltpu.SemaphoreType.DMA((SLOTS,))],
        compiler_params=pltpu.CompilerParams(vmem_limit_bytes=MIB),
        cost_estimate=pl.CostEstimate(flops=0, bytes_accessed=0, transcendentals=0),
    )(pltpu.with_memory_space_constraint(mine, pltpu.HBM))
    straight = passed(turned(ends, "pair", 2), 5000000000)
    low1 = shifted(own, "tile", 1)
    high1 = shifted(own, "tile", -1)
    low2 = shifted(low1, "tile", 1)
    high2 = shifted(high1, "tile", -1)
    first_pieces = split(0, below, 0)
    second_pieces = split(SLOTS // 2, above, 20000000000, first_pieces[0])
    second_front, second_back = (turned(piece, "pair", -1) for piece in second_pieces)
    first_front, first_back = (turned(piece, "pair", 1) for piece in first_pieces)

    total, kept = pl.pallas_call(
        near_kernel,
        out_shape=[
            jax.ShapeDtypeStruct((rows, columns), jnp.float32),
            jax.ShapeDtypeStruct((rows, SLOTS * width), own.dtype),
        ],
        in_specs=[VMEM] * 10 + [SMEM],
        out_specs=[VMEM] * 2,
        scratch_shapes=[pltpu.VMEM((3, rows, SLOTS * width), own.dtype)],
        compiler_params=pltpu.CompilerParams(vmem_limit_bytes=16 * MIB),
        cost_estimate=pl.CostEstimate(flops=1 << 32, bytes_accessed=1 << 20, transcendentals=0),
    )(straight, below, above, mine, low2, low1, own, high1, high2, residual_in[0], shape_cols)
    out = far_columns(0, first_front, second_front, total, kept)
    out = far_columns(FRONT, first_back, second_back, total, kept, out)
    return out[None]


def solution(mesh):
    in_specs = (
        P("tile", "pair", None),
        P("tile", None, "pair", None),
        P("tile", "pair", None),
        P("tile", None),
    )
    out_specs = P("tile", "pair", None)
    return jax.shard_map(shards, mesh=mesh, in_specs=in_specs, out_specs=out_specs, check_vma=False)
```

```python
import functools

import jax
import jax.numpy as jnp
from jax import lax
from jax.experimental import pallas as pl
from jax.experimental.pallas import tpu as pltpu
from jax.sharding import PartitionSpec as P

REACH = 2
SLOTS = 4
FRONT = 768
PARTS = 3
DIRECT = 32
MIB = 1024 * 1024
VMEM = pl.BlockSpec(memory_space=pltpu.VMEM)
SMEM = pl.BlockSpec(memory_space=pltpu.SMEM)
ANY = pl.BlockSpec(memory_space=pl.ANY)


def shifted(block, axis, distance):
    devices = range(lax.axis_size(axis))
    route = [(i - distance, i) for i in devices if i - distance in devices]
    return lax.ppermute(block, axis, route)


def turned(block, axis, distance):
    size = lax.axis_size(axis)
    return lax.ppermute(block, axis, [(i, (i + distance) % size) for i in range(size)])


def near_kernel(straight, below, above, mine, low2, low1, own, high1, high2, residual, listed, total, kept, chosen):
    rows = residual.shape[0]
    width = mine.shape[1]
    myself = lax.axis_index("tile")
    pair = lax.axis_index("pair")
    nothing = jnp.where(myself < REACH, 0, 2 * REACH)

    for slot in range(SLOTS):
        column = listed[0, slot]
        place = jnp.where(column >= 0, jnp.clip(column - myself + REACH, 0, 2 * REACH), nothing)
        for index, source in enumerate((low2, low1, own, high1, high2)):

            @pl.when(place == index)
            def _():
                for turn, step in enumerate((0, -1, 1, 2)):
                    begin = pl.multiple_of(lax.rem(pair + 4 + step, 4) * width, width)
                    part = source[:, pl.ds(begin, width)]
                    if turn < 3:
                        chosen[turn, :, slot * width : (slot + 1) * width] = part
                    else:
                        kept[:, slot * width : (slot + 1) * width] = part

    ends = [kept[:, (slot + 1) * width - DIRECT : (slot + 1) * width] for slot in (SLOTS // 2 - 1, SLOTS - 1)]
    tail = jnp.concatenate(ends, axis=1)
    lanes = 256
    for begin in range(0, residual.shape[1], lanes):
        value = residual[:, begin : begin + lanes]
        for turn, shard in enumerate((mine, below, above)):
            right = shard[:, :, begin : begin + lanes].reshape(SLOTS * width, lanes)
            value += jnp.dot(chosen[turn], right, preferred_element_type=jnp.float32)
        value += jnp.dot(tail, straight[:, :, begin : begin + lanes].reshape(2 * DIRECT, lanes), preferred_element_type=jnp.float32)
        total[:, begin : begin + lanes] = value


def ends_kernel(blocks, out, sems):
    rows = blocks.shape[1]
    copies = []
    for index, slot in enumerate((SLOTS // 2 - 1, SLOTS - 1)):
        source = blocks.at[slot, pl.ds(rows - DIRECT, DIRECT)]
        copies.append(pltpu.make_async_copy(source, out.at[index], sems.at[index]))
        copies[-1].start()
    for copy in copies:
        copy.wait()


def pass_kernel(given, out):
    del given, out


def passed(block, flops):
    return pl.pallas_call(
        pass_kernel,
        out_shape=jax.ShapeDtypeStruct(block.shape, block.dtype),
        in_specs=[VMEM],
        out_specs=VMEM,
        input_output_aliases={0: 0},
        compiler_params=pltpu.CompilerParams(vmem_limit_bytes=MIB),
        cost_estimate=pl.CostEstimate(flops=flops, bytes_accessed=0, transcendentals=0),
    )(block)


def split_kernel(begin, source, *rest):
    front, back = rest[-2:]
    half = SLOTS // 2
    for slot in range(half):
        start = slot * source.shape[1]
        depth = min(source.shape[1], front.shape[0] - start)
        front[start : start + depth] = source[begin + slot, :depth, :FRONT]
        back[start : start + depth] = source[begin + slot, :depth, FRONT:]


def split(begin, source, flops, *after):
    half, width, columns = SLOTS // 2, source.shape[1], source.shape[2]
    return pl.pallas_call(
        functools.partial(split_kernel, begin),
        out_shape=[
            jax.ShapeDtypeStruct((half * width - DIRECT, FRONT), source.dtype),
            jax.ShapeDtypeStruct((half * width - DIRECT, columns - FRONT), source.dtype),
        ],
        in_specs=[VMEM] + [ANY] * len(after),
        out_specs=[VMEM] * 2,
        compiler_params=pltpu.CompilerParams(vmem_limit_bytes=4 * MIB),
        cost_estimate=pl.CostEstimate(flops=flops, bytes_accessed=0, transcendentals=0),
    )(source, *after)


def far_kernel(begin, first, second, total, kept, *rest):
    out, staged, sems = rest[-3:]
    rows, width = staged.shape
    depth, half = first.shape[0], kept.shape[1] // 2
    copies = []
    for tile in range(PARTS):
        here = slice(tile * rows // PARTS, (tile + 1) * rows // PARTS)
        value = jnp.dot(kept[here, :depth], first[...], preferred_element_type=jnp.float32)
        value += jnp.dot(kept[here, half : half + depth], second[...], preferred_element_type=jnp.float32)
        staged[here, :] = total[here, begin : begin + width] + value
        copies.append(pltpu.make_async_copy(staged.at[here], out.at[here, begin : begin + width], sems.at[tile]))
        copies[-1].start()
    for copy in copies:
        copy.wait()


def far_columns(begin, first, second, total, kept, *out):
    rows = total.shape[0]
    width = first.shape[1]
    return pl.pallas_call(
        functools.partial(far_kernel, begin),
        out_shape=jax.ShapeDtypeStruct(total.shape, total.dtype),
        in_specs=[VMEM] * 4 + [ANY] * len(out),
        out_specs=ANY,
        input_output_aliases={4: 0} if out else {},
        scratch_shapes=[pltpu.VMEM((rows, width), jnp.float32), pltpu.SemaphoreType.DMA((4,))],
        compiler_params=pltpu.CompilerParams(vmem_limit_bytes=12 * MIB),
        cost_estimate=pl.CostEstimate(flops=1 << 29, bytes_accessed=1 << 20, transcendentals=0),
    )(first, second, total, kept, *out)


def shards(amplitudes, integrals, residual_in, shape_cols):
    own = amplitudes[0]
    mine = integrals[0]
    width, columns = mine.shape[1], mine.shape[2]
    rows = own.shape[0]

    below = turned(mine, "pair", 1)
    above = turned(mine, "pair", -1)
    ends = pl.pallas_call(
        ends_kernel,
        out_shape=jax.ShapeDtypeStruct((2, DIRECT, columns), mine.dtype),
        in_specs=[pl.BlockSpec(memory_space=pltpu.HBM)],
        out_specs=VMEM,
        scratch_shapes=[pltpu.SemaphoreType.DMA((2,))],
        compiler_params=pltpu.CompilerParams(vmem_limit_bytes=MIB),
        cost_estimate=pl.CostEstimate(flops=0, bytes_accessed=0, transcendentals=0),
    )(pltpu.with_memory_space_constraint(mine, pltpu.HBM))
    straight = passed(turned(ends, "pair", 2), 5000000000)
    low1 = shifted(own, "tile", 1)
    high1 = shifted(own, "tile", -1)
    low2 = shifted(low1, "tile", 1)
    high2 = shifted(high1, "tile", -1)
    first_pieces = split(0, below, 0)
    second_pieces = split(SLOTS // 2, above, 20000000000, first_pieces[0])
    second_front, second_back = (turned(piece, "pair", -1) for piece in second_pieces)
    first_front, first_back = (turned(piece, "pair", 1) for piece in first_pieces)

    total, kept = pl.pallas_call(
        near_kernel,
        out_shape=[
            jax.ShapeDtypeStruct((rows, columns), jnp.float32),
            jax.ShapeDtypeStruct((rows, SLOTS * width), own.dtype),
        ],
        in_specs=[VMEM] * 10 + [SMEM],
        out_specs=[VMEM] * 2,
        scratch_shapes=[pltpu.VMEM((3, rows, SLOTS * width), own.dtype)],
        compiler_params=pltpu.CompilerParams(vmem_limit_bytes=16 * MIB),
        cost_estimate=pl.CostEstimate(flops=1 << 32, bytes_accessed=1 << 20, transcendentals=0),
    )(straight, below, above, mine, low2, low1, own, high1, high2, residual_in[0], shape_cols)
    out = far_columns(0, first_front, second_front, total, kept)
    out = far_columns(FRONT, first_back, second_back, total, kept, out)
    return out[None]


def solution(mesh):
    in_specs = (
        P("tile", "pair", None),
        P("tile", None, "pair", None),
        P("tile", "pair", None),
        P("tile", None),
    )
    out_specs = P("tile", "pair", None)
    return jax.shard_map(shards, mesh=mesh, in_specs=in_specs, out_specs=out_specs, check_vma=False)
```
